32 devices in a mesh: seq: 8 (over z, y), head: 4 (over x, core).
Axes of the slice: x: 2, y: 2, z: 4, core: 2. Of those that a mesh axis runs over, the one named last changes fastest.
Arguments:
- tokens: bfloat16 [8192, 2048], P('seq'), may hold values from -26 to 26, as said below
- w_query: bfloat16 [2048, 2048], P(None, 'head'), as said below
- w_key: bfloat16 [2048, 2048], P(None, 'head'), as said below
- w_value: bfloat16 [2048, 2048], P(None, 'head'), may hold values from -0.125 to 0.125
- w_out: bfloat16 [2048, 2048], P('head'), may hold values from -0.125 to 0.125
- window_blocks: int32 [64, 3], P('seq'), may hold values from 0 to 63, as said below
- random_blocks: int32 [64, 4], replicated, may hold values from 0 to 63, as said below
- summary_blocks: int32 [64, 2], P('seq'), may hold values from 0 to 3
- seg_start: int32 [512], replicated, may hold values from 0 to 8191, as said below
- seg_end: int32 [512], replicated, may hold values from 1 to 8192, as said below
Outputs:
- mixed: bfloat16 [8192, 2048], P('seq', 'head')
The draws below stay inside these ranges and needn't reach their ends.
Inputs may be any that keep to these rules, and one draw needn't show every extreme that they name: `tokens`: finite activations. `w_query`: a projection scaled by its fan-in. `w_key`: a projection scaled by its fan-in. `window_blocks`: row i names block i first, then two other blocks at most 2 blocks away from i. `random_blocks`: in the rows of one index of seq (aligned runs of 8 rows), the blocks held by any one index of seq are named at most 6 times, and those of some index exactly 6 times. `seg_start`: each segment holds 1 to 512 tokens, segment 0 exactly 512; segment s lies within the tokens of one index of seq, namely index (s // 64 + 4) mod 8. seg_end is greater than seg_start and at most seg_start + 512.
All inputs are finite; a program needn't handle non-finite values.
Results may differ from the reference program's by a relative error of at most 0.0095.
Values may be sent and summed in bfloat16 or wider, within the bound.
No kernel may reach another device: no remote copies, remote signals or barrier semaphores. Data moves between devices by JAX's collectives and lax.ppermute only.
A program may use at most 192 MiB of HBM per device.

```python
import jax
import jax.numpy as jnp
from jax import lax

D = 2048
H = 16
HD = 128
BLK = 128
NB_DEV = 8
R = 4
FIXL = 2
NSB = 4
MAXSEG = 512
S_DEV = 1024
TOKENS = 8192
NBLOCKS = 64
NSUM = 512
CAP = 6
N_HEAD = 4


def draw_tokens(key, part):
    base_draw = jnp.clip(jax.random.normal(jax.random.fold_in(key, 1), (TOKENS, D), jnp.float32), -6.0, 6.0)
    return base_draw.astype(jnp.bfloat16)


def query_base(key):
    return jnp.clip(jax.random.normal(jax.random.fold_in(key, 11), (D, H * HD), jnp.float32), -6.0, 6.0) * D ** (-0.5)


def draw_w_query(key, part):
    return query_base(key).astype(jnp.bfloat16)


def draw_w_key(key, part):
    own_part = jnp.clip(jax.random.normal(jax.random.fold_in(key, 12), (D, H * HD), jnp.float32), -6.0, 6.0) * D ** (-0.5)
    return own_part.astype(jnp.bfloat16)


def draw_window_blocks(key, part):
    block_ids = jnp.arange(NBLOCKS, dtype=jnp.int32)
    offsets = jnp.array([-2, -1, 1, 2], jnp.int32)
    target = block_ids[:, None] + offsets[None, :]
    usable = ((target >= 0) & (target < NBLOCKS)).astype(jnp.int32)
    priority = jax.random.randint(key, (NBLOCKS, 4), 0, 1024) * 4 + jnp.arange(4, dtype=jnp.int32)[None, :] + usable * 8192
    ordering = jnp.argsort(-priority, axis=1)
    picked = jnp.take_along_axis(target, ordering[:, :2], axis=1)
    return jnp.concatenate([block_ids[:, None], picked], axis=1).astype(jnp.int32)


def owners_of(key):
    devices = NBLOCKS // NB_DEV
    ref_count = NB_DEV * R

    def one_device(dev_key):
        first_owner = jax.random.randint(jax.random.fold_in(dev_key, 1), (), 0, devices)
        shuffled = jax.random.permutation(jax.random.fold_in(dev_key, 2), (devices - 1) * CAP)
        others = shuffled // CAP
        others = others + (others >= first_owner).astype(jnp.int32)
        chosen = jnp.concatenate([jnp.full((CAP,), first_owner, jnp.int32), others[:ref_count - CAP].astype(jnp.int32)])
        return jax.random.permutation(jax.random.fold_in(dev_key, 3), chosen)
    key_list = jax.random.split(key, devices)
    return jax.vmap(one_device)(key_list)


def draw_random_blocks(key, part):
    owners = owners_of(jax.random.fold_in(key, 31))
    local_ids = jax.random.randint(jax.random.fold_in(key, 32), owners.shape, 0, NB_DEV)
    return (owners * NB_DEV + local_ids).reshape(NBLOCKS, R).astype(jnp.int32)


def segment_pair(key):
    devices = NBLOCKS // NB_DEV
    share_rows = NSUM // devices
    row_ids = jnp.arange(NSUM, dtype=jnp.int32)
    home = (row_ids // share_rows + devices // 2) % devices
    raw = jax.random.randint(jax.random.fold_in(key, 2), (NSUM,), 0, MAXSEG)
    span_rows = 1 + raw * raw // MAXSEG
    span_rows = jnp.where(row_ids == 0, MAXSEG, span_rows).astype(jnp.int32)
    draw_offset = jax.random.randint(jax.random.fold_in(key, 1), (NSUM,), 0, S_DEV + 1)
    room = S_DEV - span_rows + 1
    offset_rows = draw_offset % room
    start_rows = home * S_DEV + offset_rows
    return (start_rows.astype(jnp.int32), (start_rows + span_rows).astype(jnp.int32))


def draw_seg_start(key, part):
    return segment_pair(jax.random.fold_in(key, 41))[0]


def draw_seg_end(key, part):
    return segment_pair(jax.random.fold_in(key, 41))[1]


def plant(entries, own_key, least, high):
    longest = entries.shape.index(max(entries.shape))
    spots = []
    for shift in (0, 1):
        where = [jax.random.randint(jax.random.fold_in(own_key, axis), (), 0, length) for axis, length in enumerate(entries.shape)]
        where[longest] = (where[longest] + shift) % entries.shape[longest]
        spots.append(tuple(where))
    return entries.at[spots[0]].set(least).at[spots[1]].set(high)


def levels(own_key, extent, cuts, least, largest):
    def one(axis_at, blocks):
        draws = jax.random.uniform(jax.random.fold_in(jax.random.fold_in(own_key, 6), axis_at), (blocks,), jnp.float32, least / len(cuts), largest / len(cuts))
        return jnp.repeat(jnp.exp(draws), extent[axis_at] // blocks).reshape((-1,) + (1,) * (len(extent) - axis_at - 1))

    gain = one(*cuts[0])
    for cut in cuts[1:]:
        gain = gain * one(*cut)
    return gain


def bell_draw(own_key, extent, scale, reach, cuts=(), kind=jnp.bfloat16):
    values = scale * jax.random.normal(own_key, extent, jnp.float32)
    if cuts:
        values = values * levels(own_key, extent, cuts, -0.22, 0.18)
    return jnp.clip(values, -reach, reach).astype(kind)


def setup_inputs(seed: int = 0) -> dict:
    seeds = jax.random.split(jax.random.key(seed), 11)
    tokens = draw_tokens(jax.random.fold_in(seeds[10], 71), 0)
    w_query = draw_w_query(jax.random.fold_in(seeds[10], 71), 0)
    w_key = draw_w_key(jax.random.fold_in(seeds[10], 71), 0)
    w_value = bell_draw(seeds[3], (D, H * HD), D ** -0.5, 0.125, ((1, 4),))
    w_out = bell_draw(seeds[4], (H * HD, D), (H * HD) ** -0.5, 0.125, ((0, 4),))
    window_blocks = draw_window_blocks(jax.random.fold_in(seeds[10], 71), 0)
    random_blocks = draw_random_blocks(jax.random.fold_in(seeds[10], 71), 0)
    summary_blocks = plant(jax.random.randint(seeds[7], (NBLOCKS, FIXL), 0, NSB), jax.random.fold_in(seeds[7], 1), 0, NSB - 1).astype(jnp.int32)
    seg_start = draw_seg_start(jax.random.fold_in(seeds[10], 71), 0)
    seg_end = draw_seg_end(jax.random.fold_in(seeds[10], 71), 0)
    return {"tokens": tokens, "w_query": w_query, "w_key": w_key, "w_value": w_value, "w_out": w_out, "window_blocks": window_blocks, "random_blocks": random_blocks, "summary_blocks": summary_blocks, "seg_start": seg_start, "seg_end": seg_end}


def project(tokens, weight):
    return jnp.dot(tokens, weight, preferred_element_type=jnp.float32).astype(jnp.bfloat16)


def reference(tokens, w_query, w_key, w_value, w_out, window_blocks, random_blocks, summary_blocks, seg_start, seg_end):
    columns = H * HD
    queries = project(tokens, w_query)
    key_rows = project(tokens, w_key)
    values = project(tokens, w_value)
    key_value = jnp.concatenate([key_rows, values], axis=1)
    padded_rows = jnp.concatenate([key_value, jnp.zeros((MAXSEG, 2 * columns), key_value.dtype)], axis=0)

    def pool(inputs):
        first_row, last_row = inputs
        window = lax.dynamic_slice_in_dim(padded_rows, first_row.astype(jnp.int32), MAXSEG, 0).astype(jnp.float32)
        inside = ((first_row.astype(jnp.int32) + jnp.arange(MAXSEG, dtype=jnp.int32)) < last_row.astype(jnp.int32)).astype(jnp.float32)
        counts = (last_row - first_row).astype(jnp.float32)
        return jnp.sum(window * inside[:, None], axis=0) / counts

    summary = lax.map(pool, (seg_start, seg_end)).astype(jnp.bfloat16).reshape(NSB, BLK, 2, columns)
    blocks = key_value.reshape(NBLOCKS, BLK, 2, columns)
    score_scale = HD ** -0.5

    def attend(inputs):
        block_queries, window_ids, random_ids, summary_ids = inputs
        gathered = jnp.concatenate([blocks[window_ids], blocks[random_ids], summary[summary_ids]], axis=0)
        gathered = gathered.reshape(-1, 2, H, HD).astype(jnp.float32)
        lifted = block_queries.reshape(BLK, H, HD).astype(jnp.float32)
        scores = jnp.einsum("qhd,khd->hqk", lifted, gathered[:, 0], precision=lax.Precision.HIGHEST) * score_scale
        row_peak = jnp.max(scores, axis=-1, keepdims=True)
        weights = jnp.exp(scores - row_peak)
        row_total = jnp.sum(weights, axis=-1)
        rounded = lax.optimization_barrier(weights.astype(jnp.bfloat16)).astype(jnp.float32)
        mixed = jnp.einsum("hqk,khd->qhd", rounded, gathered[:, 1], precision=lax.Precision.HIGHEST)
        mixed = mixed / jnp.transpose(row_total)[:, :, None]
        return mixed.reshape(BLK, columns).astype(jnp.bfloat16)

    attended = lax.map(attend, (queries.reshape(NBLOCKS, BLK, columns), window_blocks, random_blocks, summary_blocks))
    attended = attended.reshape(TOKENS, columns)
    group_cols = columns // N_HEAD
    out_sum = jnp.zeros((TOKENS, D), jnp.float32)
    for group_idx in range(N_HEAD):
        lower = group_idx * group_cols
        partial_value = jnp.dot(attended[:, lower:lower + group_cols], w_out[lower:lower + group_cols], preferred_element_type=jnp.float32)
        out_sum = out_sum + lax.optimization_barrier(partial_value.astype(jnp.bfloat16)).astype(jnp.float32)
    return out_sum.astype(jnp.bfloat16)
```

```python
import functools

import jax
import jax.numpy as jnp
import numpy as np
from jax import lax
from jax.experimental import pallas as pl
from jax.experimental.pallas import tpu as pltpu
from jax.sharding import PartitionSpec as P

HD = 128
BLK = 128
MIB = 1 << 20


def ring_order(devices):
    half = devices // 2
    return [2 * i for i in range(half)] + [2 * i + 1 for i in reversed(range(half))]


def kv_kernel(tokens_ref, wk_ref, wv_ref, start_ref, end_ref, out_ref):
    tok_rows = tokens_ref.shape[0]
    share = start_ref.shape[0]
    weight = jnp.concatenate([wk_ref[...], wv_ref[...]], axis=1)
    kv = jnp.dot(tokens_ref[...], weight, preferred_element_type=jnp.float32).astype(jnp.bfloat16)
    out_ref[:tok_rows, :] = kv
    position = lax.broadcasted_iota(jnp.int32, (share, tok_rows), 1)
    start = start_ref[...]
    end = end_ref[...]
    member = ((position >= start) & (position < end)).astype(jnp.float32).astype(jnp.bfloat16)
    sums = jnp.dot(member, kv, preferred_element_type=jnp.float32)
    counts = (end - start).astype(jnp.float32)
    out_ref[tok_rows:, :] = (sums / counts).astype(jnp.bfloat16)


def project_kv(tokens, w_key, w_value, start, end, head):
    tok_rows, width = tokens.shape
    share = start.shape[0]
    return pl.pallas_call(
        kv_kernel,
        grid=(1,),
        in_specs=[
            pl.BlockSpec((tok_rows, width), lambda i: (0, 0)),
            pl.BlockSpec((width, HD), lambda i: (0, head)),
            pl.BlockSpec((width, HD), lambda i: (0, head)),
            pl.BlockSpec((share, 1), lambda i: (0, 0)),
            pl.BlockSpec((share, 1), lambda i: (0, 0)),
        ],
        out_specs=pl.BlockSpec((tok_rows + share, 2 * HD), lambda i: (0, 0)),
        out_shape=jax.ShapeDtypeStruct((tok_rows + share, 2 * HD), jnp.bfloat16),
        compiler_params=pltpu.CompilerParams(vmem_limit_bytes=40 * MIB),
        cost_estimate=pl.CostEstimate(
            flops=2 * tok_rows * width * 2 * HD, bytes_accessed=6 * MIB, transcendentals=0
        ),
        name="project_kv",
    )(tokens, w_key, w_value, start, end)


def attend_kernel(devices, table_ref, owner_ref, q_ref, *refs):
    buffers = refs[: devices + 1]
    out_ref, kv, summary, sems = refs[devices + 1 :]
    tok_rows = q_ref.shape[0]
    half = tok_rows // 2
    share = summary.shape[0] // devices
    copies = []

    def copy(source, target):
        done = pltpu.make_async_copy(source, target, sems.at[len(copies)])
        done.start()
        copies.append(done)

    for at, buffer in enumerate(buffers):
        owner = owner_ref[min(at, devices - 1)]
        first = half if at == devices else 0
        rows = tok_rows if at < devices - 1 else half
        base = pl.multiple_of(owner * tok_rows + first, BLK)
        copy(buffer.at[pl.ds(0, rows)], kv.at[pl.ds(base, rows)])
        if at != devices - 1:
            segment = lax.rem(owner + devices // 2, devices)
            base = pl.multiple_of(segment * share, 16)
            copy(buffer.at[pl.ds(rows, share)], summary.at[pl.ds(base, share)])
    for done in copies:
        done.wait()
    factor = HD**-0.5 * float(np.log2(np.e))
    slots = table_ref.shape[1]

    def one_block(block, carry):
        parts = []
        for slot in range(slots):
            base = pl.multiple_of(table_ref[block, slot] * BLK, BLK)
            source = kv if slot < slots - 2 else summary
            parts.append(source[pl.ds(base, BLK), :])
        gathered = jnp.concatenate(parts, axis=0)
        rows = pl.ds(pl.multiple_of(block * BLK, BLK), BLK)
        scores = lax.dot_general(
            q_ref[rows, :],
            gathered[:, :HD],
            (((1,), (1,)), ((), ())),
            preferred_element_type=jnp.float32,
        )
        peak = jnp.max(scores, axis=1, keepdims=True)
        weights = jnp.exp2((scores - peak) * factor)
        total = jnp.sum(weights, axis=1, keepdims=True)
        mixed = jnp.dot(
            weights.astype(jnp.bfloat16), gathered[:, HD:], preferred_element_type=jnp.float32
        )
        out_ref[rows, :] = (mixed / total).astype(jnp.bfloat16)
        return carry

    lax.fori_loop(0, tok_rows // BLK, one_block, 0)


def attend(table, owner_ids, queries, buffers, head, devices, share):
    tok_rows = queries.shape[0]
    any_spec = pl.BlockSpec(memory_space=pl.ANY)
    smem = pl.BlockSpec(memory_space=pltpu.SMEM)
    return pl.pallas_call(
        functools.partial(attend_kernel, devices),
        grid=(1,),
        in_specs=[smem, smem, pl.BlockSpec((tok_rows, HD), lambda i: (0, head))]
        + [any_spec] * len(buffers),
        out_specs=pl.BlockSpec((tok_rows, HD), lambda i: (0, 0)),
        out_shape=jax.ShapeDtypeStruct((tok_rows, HD), jnp.bfloat16),
        scratch_shapes=[
            pltpu.VMEM((devices * tok_rows, 2 * HD), jnp.bfloat16),
            pltpu.VMEM((devices * share, 2 * HD), jnp.bfloat16),
            pltpu.SemaphoreType.DMA((2 * devices + 1,)),
        ],
        compiler_params=pltpu.CompilerParams(vmem_limit_bytes=48 * MIB),
        cost_estimate=pl.CostEstimate(
            flops=4 * tok_rows * 1152 * HD,
            bytes_accessed=devices * tok_rows * 4 * HD,
            transcendentals=tok_rows * 1152,
        ),
        name="attend",
    )(table, owner_ids, queries, *buffers)


def out_kernel(pieces, *refs):
    w_ref, out_ref = refs[pieces:]
    rows = jnp.concatenate([ref[...] for ref in refs[:pieces]], axis=1)
    out_ref[...] = jnp.dot(rows, w_ref[...], preferred_element_type=jnp.float32).astype(
        jnp.bfloat16
    )


def project_out(pieces, weight):
    tok_rows = pieces[0].shape[0]
    width, columns = weight.shape
    tile = 256
    return pl.pallas_call(
        functools.partial(out_kernel, len(pieces)),
        grid=(tok_rows // tile,),
        in_specs=[pl.BlockSpec((tile, HD), lambda i: (i, 0))] * len(pieces)
        + [pl.BlockSpec((width, columns), lambda i: (0, 0))],
        out_specs=pl.BlockSpec((tile, columns), lambda i: (i, 0)),
        out_shape=jax.ShapeDtypeStruct((tok_rows, columns), jnp.bfloat16),
        compiler_params=pltpu.CompilerParams(vmem_limit_bytes=40 * MIB),
        cost_estimate=pl.CostEstimate(
            flops=2 * tok_rows * width * columns, bytes_accessed=7 * MIB, transcendentals=0
        ),
        name="project_out",
    )(*pieces, weight)


def ring_gather(chunk, tok_rows, devices):
    order = ring_order(devices)
    forward = [(order[p], order[(p + 1) % devices]) for p in range(devices)]
    backward = [(target, source) for source, target in forward]
    buffers = [chunk]
    ahead = behind = chunk
    for _ in range(1, devices // 2):
        ahead = lax.ppermute(ahead, "seq", forward)
        behind = lax.ppermute(behind, "seq", backward)
        buffers += [ahead, behind]
    half = tok_rows // 2
    buffers.append(lax.ppermute(ahead[:half], "seq", forward))
    buffers.append(lax.ppermute(behind[half:], "seq", backward))
    return buffers


def per_device(
    tokens,
    w_query,
    w_key,
    w_value,
    w_out,
    window_blocks,
    random_blocks,
    summary_blocks,
    seg_start,
    seg_end,
):
    tok_rows = tokens.shape[0]
    columns = w_query.shape[1]
    heads = columns // HD
    block_count = tok_rows // BLK
    devices = lax.axis_size("seq")
    groups = lax.axis_size("head")
    me = lax.axis_index("seq")
    group = lax.axis_index("head")
    share = seg_start.shape[0] // devices

    order = np.array(ring_order(devices), np.int32)
    position = jnp.asarray(np.argsort(order).astype(np.int32))[me]
    steps = [0] + [s * k for k in range(1, devices // 2) for s in (-1, 1)] + [devices // 2]
    owner_ids = jnp.asarray(order)[(position + jnp.asarray(steps, jnp.int32)) % devices]
    mine = lax.dynamic_slice_in_dim(random_blocks, me * block_count, block_count, 0)
    table = jnp.concatenate([window_blocks, mine, summary_blocks], axis=1)
    first_segment = lax.rem(me + devices // 2, devices) * share
    start = lax.dynamic_slice_in_dim(seg_start, first_segment, share, 0) - me * tok_rows
    end = lax.dynamic_slice_in_dim(seg_end, first_segment, share, 0) - me * tok_rows

    gathered = [
        ring_gather(
            project_kv(tokens, w_key, w_value, start[:, None], end[:, None], head),
            tok_rows,
            devices,
        )
        for head in range(heads)
    ]
    queries = jnp.dot(tokens, w_query, preferred_element_type=jnp.float32).astype(jnp.bfloat16)

    out_weight = lax.all_to_all(
        w_out.reshape(heads * HD, groups, -1), "head", split_axis=1, concat_axis=0, tiled=True
    ).reshape(groups, heads * HD, -1)
    across = [(g, g ^ 2) for g in range(groups)]
    beside = [(g, g ^ 1) for g in range(groups)]
    pieces = []
    weights = []
    for head in range(heads):
        own = attend(table, owner_ids, queries, gathered[head], head, devices, share)
        other = lax.ppermute(own, "head", across)
        pieces += [own, other, lax.ppermute(own, "head", beside), lax.ppermute(other, "head", beside)]
        for flip in (0, 2, 1, 3):
            rows = lax.dynamic_index_in_dim(out_weight, group ^ flip, 0, keepdims=False)
            weights.append(rows[head * HD : (head + 1) * HD])
    return project_out(pieces, jnp.concatenate(weights, axis=0))


def solution(mesh):
    placed = (
        P("seq", None),
        P(None, "head"),
        P(None, "head"),
        P(None, "head"),
        P("head", None),
        P("seq", None),
        P(),
        P("seq", None),
        P(),
        P(),
    )
    return jax.shard_map(
        per_device, mesh=mesh, in_specs=placed, out_specs=P("seq", "head"), check_vma=False
    )
```

```python
import functools

import jax
import jax.numpy as jnp
import numpy as np
from jax import lax
from jax.experimental import pallas as pl
from jax.experimental.pallas import tpu as pltpu
from jax.sharding import PartitionSpec as P

HD = 128
BLK = 128
MIB = 1 << 20


def ring_order(devices):
    half = devices // 2
    return [2 * i for i in range(half)] + [2 * i + 1 for i in reversed(range(half))]


def kv_kernel(token_rows, heads, tokens_ref, wk_ref, wv_ref, start_ref, end_ref, own_ref, chunk_ref, w_ref):
    tok_rows = tokens_ref.shape[0]
    share = start_ref.shape[0]
    for head in range(heads):
        at = slice(head * HD, (head + 1) * HD)
        w_ref[:, 2 * head * HD : (2 * head + 1) * HD] = wk_ref[:, at]
        w_ref[:, (2 * head + 1) * HD : (2 * head + 2) * HD] = wv_ref[:, at]
    kv = jnp.dot(tokens_ref[...], w_ref[...], preferred_element_type=jnp.float32)
    kv = kv.astype(jnp.bfloat16)
    own_ref[...] = kv[:token_rows]
    chunk_ref[: tok_rows - token_rows, :] = kv[token_rows:]
    position = lax.broadcasted_iota(jnp.int32, (share, tok_rows), 1)
    start = start_ref[...]
    end = end_ref[...]
    member = ((position >= start) & (position < end)).astype(jnp.float32).astype(jnp.bfloat16)
    sums = jnp.dot(member, kv, preferred_element_type=jnp.float32)
    counts = (end - start).astype(jnp.float32)
    chunk_ref[tok_rows - token_rows :, :] = (sums / counts).astype(jnp.bfloat16)


def project_kv(tokens, w_key, w_value, start, end, token_rows, group, heads):
    tok_rows, width = tokens.shape
    share = start.shape[0]
    columns = 2 * heads * HD
    sent = tok_rows - token_rows + share
    return pl.pallas_call(
        functools.partial(kv_kernel, token_rows, heads),
        grid=(1,),
        in_specs=[
            pl.BlockSpec((tok_rows, width), lambda i: (0, 0)),
            pl.BlockSpec((width, heads * HD), lambda i: (0, group)),
            pl.BlockSpec((width, heads * HD), lambda i: (0, group)),
            pl.BlockSpec((share, 1), lambda i: (0, 0)),
            pl.BlockSpec((share, 1), lambda i: (0, 0)),
        ],
        out_specs=[
            pl.BlockSpec((token_rows, columns), lambda i: (0, 0)),
            pl.BlockSpec((sent, columns), lambda i: (0, 0)),
            pl.BlockSpec((width, columns), lambda i: (0, 0)),
        ],
        out_shape=[
            jax.ShapeDtypeStruct((token_rows, columns), jnp.bfloat16),
            jax.ShapeDtypeStruct((sent, columns), jnp.bfloat16),
            jax.ShapeDtypeStruct((width, columns), jnp.bfloat16),
        ],
        compiler_params=pltpu.CompilerParams(vmem_limit_bytes=48 * MIB),
        cost_estimate=pl.CostEstimate(
            flops=2 * tok_rows * width * columns, bytes_accessed=10 * MIB, transcendentals=0
        ),
        name="project_kv",
    )(tokens, w_key, w_value, start, end)


def rows_kernel(runs, piece, count, parts, group_ref, *refs):
    sources = refs[:parts]
    weights = refs[parts : parts + count]
    outs = refs[parts + count : parts + 2 * count]
    held = refs[parts + 2 * count : 2 * parts + 2 * count]
    held_weights, sems = refs[2 * parts + 2 * count :]
    columns = held_weights.shape[1] // count
    copies = []
    for at in range(count):
        copies.append((weights[at], held_weights.at[:, pl.ds(at * columns, columns)]))
    copies += [(source, held[at]) for at, source in enumerate(sources)]
    started = []
    for at, (source, target) in enumerate(copies):
        started.append(pltpu.make_async_copy(source, target, sems.at[at]))
        started[-1].start()
    for at in range(count):
        started[at].wait()
    for at in range(parts):
        started[count + at].wait()
        rows = jnp.dot(held[at][...], held_weights[...], preferred_element_type=jnp.float32)
        rows = rows.astype(jnp.bfloat16)
        flip = at if parts == 4 else at // 2
        first = 0 if parts == 4 else (at % 2) * (piece // 2)
        slot = group_ref[flip]
        for run in range(runs):
            size = rows.shape[0] // runs
            base = pl.multiple_of(run * 4 * piece + slot * piece + first, 16)
            for to in range(count):
                outs[to][pl.ds(base, size), :] = rows[
                    run * size : (run + 1) * size, to * columns : (to + 1) * columns
                ]


def project_rows(parts, weights, slots, runs, piece):
    width = parts[0].shape[1]
    columns = weights[0].shape[1]
    count = len(weights)
    rows = runs * 4 * piece
    any_spec = pl.BlockSpec(memory_space=pl.ANY)
    return pl.pallas_call(
        functools.partial(rows_kernel, runs, piece, count, len(parts)),
        grid=(1,),
        in_specs=[pl.BlockSpec(memory_space=pltpu.SMEM)] + [any_spec] * (len(parts) + count),
        out_specs=[pl.BlockSpec((rows, columns), lambda i: (0, 0))] * count,
        out_shape=[jax.ShapeDtypeStruct((rows, columns), jnp.bfloat16)] * count,
        scratch_shapes=[pltpu.VMEM(part.shape, jnp.bfloat16) for part in parts]
        + [
            pltpu.VMEM((width, count * columns), jnp.bfloat16),
            pltpu.SemaphoreType.DMA((len(parts) + count,)),
        ],
        compiler_params=pltpu.CompilerParams(vmem_limit_bytes=48 * MIB),
        cost_estimate=pl.CostEstimate(
            flops=2 * rows * width * count * columns, bytes_accessed=12 * MIB, transcendentals=0
        ),
        name="project_rows",
    )(slots, *parts, *weights)


def attend_kernel(devices, token_rows, column, table_ref, owner_ref, q_ref, own_ref, *refs):
    buffers = refs[: devices + 1]
    steps = devices // 2
    projected = refs[devices + 1 : devices + 1 + steps]
    out_ref, kv, summary, sems = refs[devices + 1 + steps :]
    tok_rows = q_ref.shape[0]
    sent = tok_rows - token_rows
    share = summary.shape[0] // devices
    half = buffers[devices - 1].shape[0]
    columns = pl.ds(column, 2 * HD)
    copies = []

    def copy(source, first, rows, target, base):
        done = pltpu.make_async_copy(
            source.at[pl.ds(first, rows), columns],
            target.at[pl.ds(pl.multiple_of(base, 16), rows)],
            sems.at[len(copies)],
        )
        done.start()
        copies.append(done)

    copy(own_ref, 0, token_rows, kv, owner_ref[0] * tok_rows)
    for step in range(1, steps + 1):
        for run in range(2 if step < steps else 1):
            owner = owner_ref[2 * step - 1 + run]
            copy(projected[step - 1], run * token_rows, token_rows, kv, owner * tok_rows)
    for at, buffer in enumerate(buffers):
        owner = owner_ref[min(at, devices - 1)]
        first = half if at == devices else 0
        rows = half if at == devices - 1 else sent - first
        copy(buffer, 0, rows, kv, owner * tok_rows + token_rows + first)
        if at != devices - 1:
            segment = lax.rem(owner + devices // 2, devices)
            copy(buffer, rows, share, summary, segment * share)
    for done in copies:
        done.wait()
    factor = HD**-0.5 * float(np.log2(np.e))
    slots = table_ref.shape[1]

    def one_block(block, carry):
        parts = []
        for slot in range(slots):
            base = pl.multiple_of(table_ref[block, slot] * BLK, BLK)
            source = kv if slot < slots - 2 else summary
            parts.append(source[pl.ds(base, BLK), :])
        gathered = jnp.concatenate(parts, axis=0)
        rows = pl.ds(pl.multiple_of(block * BLK, BLK), BLK)
        scores = lax.dot_general(
            q_ref[rows, :],
            gathered[:, :HD],
            (((1,), (1,)), ((), ())),
            preferred_element_type=jnp.float32,
        )
        peak = jnp.max(scores, axis=1, keepdims=True)
        weights = jnp.exp2((scores - peak) * factor)
        total = jnp.sum(weights, axis=1, keepdims=True)
        mixed = jnp.dot(
            weights.astype(jnp.bfloat16), gathered[:, HD:], preferred_element_type=jnp.float32
        )
        out_ref[rows, :] = (mixed / total).astype(jnp.bfloat16)
        return carry

    lax.fori_loop(0, tok_rows // BLK, one_block, 0)


def attend(table, owner_ids, queries, own, buffers, projected, head, column, devices, share):
    tok_rows = queries.shape[0]
    any_spec = pl.BlockSpec(memory_space=pl.ANY)
    smem = pl.BlockSpec(memory_space=pltpu.SMEM)
    return pl.pallas_call(
        functools.partial(attend_kernel, devices, own.shape[0], column),
        grid=(1,),
        in_specs=[smem, smem, pl.BlockSpec((tok_rows, HD), lambda i: (0, head))]
        + [any_spec] * (1 + len(buffers) + len(projected)),
        out_specs=pl.BlockSpec((tok_rows, HD), lambda i: (0, 0)),
        out_shape=jax.ShapeDtypeStruct((tok_rows, HD), jnp.bfloat16),
        scratch_shapes=[
            pltpu.VMEM((devices * tok_rows, 2 * HD), jnp.bfloat16),
            pltpu.VMEM((devices * share, 2 * HD), jnp.bfloat16),
            pltpu.SemaphoreType.DMA((3 * devices + 1,)),
        ],
        compiler_params=pltpu.CompilerParams(vmem_limit_bytes=48 * MIB),
        cost_estimate=pl.CostEstimate(
            flops=4 * tok_rows * 1152 * HD,
            bytes_accessed=devices * tok_rows * 4 * HD,
            transcendentals=tok_rows * 1152,
        ),
        name="attend",
    )(table, owner_ids, queries, own, *buffers, *projected)


def out_kernel(pieces, *refs):
    w_ref, out_ref = refs[pieces:]
    rows = jnp.concatenate([ref[...] for ref in refs[:pieces]], axis=1)
    out_ref[...] = jnp.dot(rows, w_ref[...], preferred_element_type=jnp.float32).astype(
        jnp.bfloat16
    )


def project_out(pieces, weight):
    tok_rows = pieces[0].shape[0]
    width, columns = weight.shape
    tile = 256
    return pl.pallas_call(
        functools.partial(out_kernel, len(pieces)),
        grid=(tok_rows // tile,),
        in_specs=[pl.BlockSpec((tile, HD), lambda i: (i, 0))] * len(pieces)
        + [pl.BlockSpec((width, columns), lambda i: (0, 0))],
        out_specs=pl.BlockSpec((tile, columns), lambda i: (i, 0)),
        out_shape=jax.ShapeDtypeStruct((tok_rows, columns), jnp.bfloat16),
        compiler_params=pltpu.CompilerParams(vmem_limit_bytes=40 * MIB),
        cost_estimate=pl.CostEstimate(
            flops=2 * tok_rows * width * columns, bytes_accessed=7 * MIB, transcendentals=0
        ),
        name="project_out",
    )(*pieces, weight)


def ring_gather(chunk, half, devices):
    order = ring_order(devices)
    forward = [(order[p], order[(p + 1) % devices]) for p in range(devices)]
    backward = [(target, source) for source, target in forward]
    buffers = [chunk]
    ahead = behind = chunk
    for _ in range(1, devices // 2):
        ahead = lax.ppermute(ahead, "seq", forward)
        behind = lax.ppermute(behind, "seq", backward)
        buffers += [ahead, behind]
    buffers.append(lax.ppermute(ahead[:half], "seq", forward))
    buffers.append(lax.ppermute(behind[half:], "seq", backward))
    return buffers


def per_device(
    tokens,
    w_query,
    w_key,
    w_value,
    w_out,
    window_blocks,
    random_blocks,
    summary_blocks,
    seg_start,
    seg_end,
):
    tok_rows = tokens.shape[0]
    columns = w_query.shape[1]
    heads = columns // HD
    block_count = tok_rows // BLK
    devices = lax.axis_size("seq")
    groups = lax.axis_size("head")
    me = lax.axis_index("seq")
    group = lax.axis_index("head")
    share = seg_start.shape[0] // devices

    order = np.array(ring_order(devices), np.int32)
    position = jnp.asarray(np.argsort(order).astype(np.int32))[me]
    steps = [0] + [s * k for k in range(1, devices // 2) for s in (-1, 1)] + [devices // 2]
    owner_ids = jnp.asarray(order)[(position + jnp.asarray(steps, jnp.int32)) % devices]
    mine = lax.dynamic_slice_in_dim(random_blocks, me * block_count, block_count, 0)
    table = jnp.concatenate([window_blocks, mine, summary_blocks], axis=1)
    first_segment = lax.rem(me + devices // 2, devices) * share
    start = lax.dynamic_slice_in_dim(seg_start, first_segment, share, 0) - me * tok_rows
    end = lax.dynamic_slice_in_dim(seg_end, first_segment, share, 0) - me * tok_rows

    across = [(g, g ^ 2) for g in range(groups)]
    beside = [(g, g ^ 1) for g in range(groups)]
    token_rows = tok_rows * 5 // 8
    piece = token_rows // groups
    group_heads = 2
    slots = group ^ jnp.arange(4, dtype=jnp.int32)

    own_piece = lax.dynamic_slice_in_dim(tokens, group * piece, piece, 0)
    token_ring = ring_gather(own_piece, piece // 2, devices)
    owns, rings, weights = [], [], []
    for at in range(heads // group_heads):
        own, chunk, weight = project_kv(
            tokens, w_key, w_value, start[:, None], end[:, None], token_rows, at, group_heads
        )
        owns.append(own)
        weights.append(weight)
        rings.append(ring_gather(chunk, chunk.shape[0] // 32 * 16, devices))
    queries = jnp.dot(tokens, w_query, preferred_element_type=jnp.float32).astype(jnp.bfloat16)

    projected = []
    for step in range(1, devices // 2 + 1):
        pair = token_ring[2 * step - 1 : 2 * step + 1]
        last = step == devices // 2
        local = jnp.concatenate(pair, axis=0)
        other = lax.ppermute(local, "head", across)
        parts = [
            local,
            lax.ppermute(local, "head", beside),
            other,
            lax.ppermute(other, "head", beside),
        ]
        runs = 1 if last else 2
        projected.append(project_rows(parts, weights, slots, runs, piece))

    out_weight = lax.all_to_all(
        w_out.reshape(heads * HD, groups, -1), "head", split_axis=1, concat_axis=0, tiled=True
    ).reshape(groups, heads * HD, -1)
    pieces = []
    out_rows = []
    for head in range(heads):
        at, within = divmod(head, group_heads)
        own = attend(
            table,
            owner_ids,
            queries,
            owns[at],
            rings[at],
            [outs[at] for outs in projected],
            head,
            within * 2 * HD,
            devices,
            share,
        )
        other = lax.ppermute(own, "head", across)
        pieces += [own, other, lax.ppermute(own, "head", beside), lax.ppermute(other, "head", beside)]
        for flip in (0, 2, 1, 3):
            rows = lax.dynamic_index_in_dim(out_weight, group ^ flip, 0, keepdims=False)
            out_rows.append(rows[head * HD : (head + 1) * HD])
    return project_out(pieces, jnp.concatenate(out_rows, axis=0))


def solution(mesh):
    placed = (
        P("seq", None),
        P(None, "head"),
        P(None, "head"),
        P(None, "head"),
        P("head", None),
        P("seq", None),
        P(),
        P("seq", None),
        P(),
        P(),
    )
    return jax.shard_map(
        per_device, mesh=mesh, in_specs=placed, out_specs=P("seq", "head"), check_vma=False
    )
```

```python
import functools

import jax
import jax.numpy as jnp
import numpy as np
from jax import lax
from jax.experimental import pallas as pl
from jax.experimental.pallas import tpu as pltpu
from jax.sharding import PartitionSpec as P

HD = 128
BLK = 128
MIB = 1 << 20


def ring_order(devices):
    half = devices // 2
    return [2 * i for i in range(half)] + [2 * i + 1 for i in reversed(range(half))]


def after(value, *others):
    return lax.optimization_barrier((value, others))[0]


def kv_kernel(heads, tokens_ref, wk_ref, wv_ref, start_ref, end_ref, *refs):
    outs = refs[: len(heads)]
    rows_held, weight, sems = refs[len(heads) :]
    tok_rows = tokens_ref.shape[0]
    tiles = 4
    tile = tok_rows // tiles
    columns = weight.shape[1]
    copies = []
    for at, head in enumerate(heads):
        for which, source in enumerate((wk_ref, wv_ref)):
            copies.append(
                pltpu.make_async_copy(
                    source.at[:, pl.ds(head * HD, HD)],
                    weight.at[:, pl.ds((2 * at + which) * HD, HD)],
                    sems.at[len(copies)],
                )
            )
    for at in range(tiles):
        rows = pl.ds(at * tile, tile)
        copies.append(
            pltpu.make_async_copy(tokens_ref.at[rows], rows_held.at[rows], sems.at[len(copies)])
        )
    for copy in copies:
        copy.start()
    for copy in copies[: 2 * len(heads)]:
        copy.wait()
    share = start_ref.shape[1]
    start = start_ref[...]
    end = end_ref[...]
    ones = jnp.ones((tile, HD), jnp.bfloat16)
    sums = jnp.zeros((share, columns), jnp.float32)
    counts = jnp.zeros((share, HD), jnp.float32)
    for at in range(tiles):
        copies[2 * len(heads) + at].wait()
        rows = slice(at * tile, (at + 1) * tile)
        kv = jnp.dot(rows_held[rows, :], weight[...], preferred_element_type=jnp.float32)
        kv = kv.astype(jnp.bfloat16)
        for to, out in enumerate(outs):
            out[rows, :] = kv[:, 2 * to * HD : 2 * (to + 1) * HD]
        position = lax.broadcasted_iota(jnp.int32, (tile, share), 0) + at * tile
        member = (position >= start) & (position < end)
        member = member.astype(jnp.float32).astype(jnp.bfloat16)
        over_rows = (((0,), (0,)), ((), ()))
        sums += lax.dot_general(member, kv, over_rows, preferred_element_type=jnp.float32)
        counts += lax.dot_general(member, ones, over_rows, preferred_element_type=jnp.float32)
    means = (sums / counts[:, :1]).astype(jnp.bfloat16)
    for to, out in enumerate(outs):
        out[tok_rows:, :] = means[:, 2 * to * HD : 2 * (to + 1) * HD]


def project_kv(tokens, w_key, w_value, start, end, heads):
    tok_rows, width = tokens.shape
    share = start.shape[1]
    any_spec = pl.BlockSpec(memory_space=pl.ANY)
    out_shape = (tok_rows + share, 2 * HD)
    return pl.pallas_call(
        functools.partial(kv_kernel, heads),
        grid=(1,),
        in_specs=[any_spec] * 3 + [pl.BlockSpec((1, share), lambda i: (0, 0))] * 2,
        out_specs=[pl.BlockSpec(out_shape, lambda i: (0, 0))] * len(heads),
        out_shape=[jax.ShapeDtypeStruct(out_shape, jnp.bfloat16)] * len(heads),
        scratch_shapes=[
            pltpu.VMEM((tok_rows, width), jnp.bfloat16),
            pltpu.VMEM((width, 2 * HD * len(heads)), jnp.bfloat16),
            pltpu.SemaphoreType.DMA((2 * len(heads) + 4,)),
        ],
        compiler_params=pltpu.CompilerParams(vmem_limit_bytes=60 * MIB),
        cost_estimate=pl.CostEstimate(
            flops=2 * tok_rows * width * 2 * HD * len(heads),
            bytes_accessed=6 * MIB,
            transcendentals=0,
        ),
        name="project_kv",
    )(tokens, w_key, w_value, start, end)


def attend_kernel(devices, table_ref, owner_ref, q_ref, *refs):
    buffers = refs[:-4]
    out_ref, kv, summary, sems = refs[-4:]
    tok_rows = q_ref.shape[0]
    share = summary.shape[0] // devices
    copies = []

    def copy(source, target):
        done = pltpu.make_async_copy(source, target, sems.at[len(copies)])
        done.start()
        copies.append(done)

    for at, buffer in enumerate(buffers):
        owner = owner_ref[min(at, devices - 1)]
        first = buffers[devices - 1].shape[0] if at == devices else 0
        rows = min(buffer.shape[0], tok_rows - first)
        base = pl.multiple_of(owner * tok_rows + first, 16)
        copy(buffer.at[pl.ds(0, rows)], kv.at[pl.ds(base, rows)])
        if buffer.shape[0] > rows:
            segment = lax.rem(owner + devices // 2, devices)
            base = pl.multiple_of(segment * share, 16)
            copy(buffer.at[pl.ds(rows, share)], summary.at[pl.ds(base, share)])
    for done in copies:
        done.wait()
    factor = HD**-0.5 * float(np.log2(np.e))
    slots = table_ref.shape[1]
    for block in range(tok_rows // BLK):
        parts = []
        for slot in range(slots):
            base = pl.multiple_of(table_ref[block, slot] * BLK, BLK)
            source = kv if slot < slots - 2 else summary
            parts.append(source[pl.ds(base, BLK), :])
        gathered = jnp.concatenate(parts, axis=0)
        rows = slice(block * BLK, (block + 1) * BLK)
        scores = lax.dot_general(
            gathered[:, :HD],
            q_ref[rows, :],
            (((1,), (1,)), ((), ())),
            preferred_element_type=jnp.float32,
        )
        peak = jnp.max(scores, axis=0, keepdims=True)
        weights = jnp.exp2((scores - peak) * factor)
        total = jnp.sum(weights, axis=0, keepdims=True)
        mixed = lax.dot_general(
            gathered[:, HD:],
            weights.astype(jnp.bfloat16),
            (((0,), (0,)), ((), ())),
            preferred_element_type=jnp.float32,
        )
        out_ref[rows, :] = (mixed / total).T.astype(jnp.bfloat16)


def attend(table, owner_ids, queries, buffers, head, devices, share):
    tok_rows = queries.shape[0]
    any_spec = pl.BlockSpec(memory_space=pl.ANY)
    smem = pl.BlockSpec(memory_space=pltpu.SMEM)
    return pl.pallas_call(
        functools.partial(attend_kernel, devices),
        grid=(1,),
        in_specs=[smem, smem, pl.BlockSpec((tok_rows, HD), lambda i: (0, head))]
        + [any_spec] * len(buffers),
        out_specs=pl.BlockSpec((tok_rows, HD), lambda i: (0, 0)),
        out_shape=jax.ShapeDtypeStruct((tok_rows, HD), jnp.bfloat16),
        scratch_shapes=[
            pltpu.VMEM((devices * tok_rows, 2 * HD), jnp.bfloat16),
            pltpu.VMEM((devices * share, 2 * HD), jnp.bfloat16),
            pltpu.SemaphoreType.DMA((2 * devices + 1,)),
        ],
        compiler_params=pltpu.CompilerParams(vmem_limit_bytes=48 * MIB),
        cost_estimate=pl.CostEstimate(
            flops=4 * tok_rows * 1152 * HD,
            bytes_accessed=devices * tok_rows * 4 * HD,
            transcendentals=tok_rows * 1152,
        ),
        name="attend",
    )(table, owner_ids, queries, *buffers)


def out_kernel(pieces, final, *refs):
    out_ref = refs[-1]
    rows = jnp.concatenate([ref[...] for ref in refs[:pieces]], axis=1)
    weights = refs[pieces : 2 * pieces]
    weight = jnp.concatenate([ref[...] for ref in weights], axis=0)
    total = jnp.dot(rows, weight, preferred_element_type=jnp.float32)
    if final:
        total += refs[2 * pieces][...]
    out_ref[...] = total.astype(out_ref.dtype)


def project_out(pieces, weights, places, total):
    tok_rows = pieces[0].shape[0]
    columns = weights[0].shape[1]
    final = total is not None
    tile = tok_rows if final else 256
    row_spec = pl.BlockSpec((tile, columns), lambda i: (i, 0))

    def weight_spec(head):
        return pl.BlockSpec((HD, columns), lambda i: (head, 0))

    return pl.pallas_call(
        functools.partial(out_kernel, len(pieces), final),
        grid=(tok_rows // tile,),
        in_specs=[pl.BlockSpec((tile, HD), lambda i: (i, 0))] * len(pieces)
        + [weight_spec(head) for _, head in places]
        + [row_spec] * final,
        out_specs=row_spec,
        out_shape=jax.ShapeDtypeStruct(
            (tok_rows, columns), jnp.bfloat16 if final else jnp.float32
        ),
        compiler_params=pltpu.CompilerParams(vmem_limit_bytes=63 * MIB),
        cost_estimate=pl.CostEstimate(
            flops=2 * tok_rows * len(pieces) * HD * columns,
            bytes_accessed=6 * MIB,
            transcendentals=0,
        ),
        name="project_out",
    )(*pieces, *[weights[at] for at, _ in places], *([total] if final else []))


WAYS = ("ahead", "behind", "both", "both")


class Ring:
    def __init__(self, chunk, devices, last_way):
        order = ring_order(devices)
        self.forward = [(order[p], order[(p + 1) % devices]) for p in range(devices)]
        self.backward = [(target, source) for source, target in self.forward]
        self.steps = devices // 2
        self.last_way = last_way
        self.buffers = [chunk]
        self.last = (chunk, chunk)

    def step(self, *others):
        ahead, behind = after(self.last, *others)
        ways = ("ahead", "behind")
        if len(self.buffers) == 2 * self.steps - 1:
            if self.last_way in ways:
                ways = (self.last_way,)
            else:
                half = ahead.shape[0] // 32 * 16
                ahead, behind = ahead[:half], behind[half:]
        given = []
        if "ahead" in ways:
            given.append(lax.ppermute(ahead, "seq", self.forward))
        if "behind" in ways:
            given.append(lax.ppermute(behind, "seq", self.backward))
        self.last = given
        self.buffers += given
        return given


def per_device(
    tokens,
    w_query,
    w_key,
    w_value,
    w_out,
    window_blocks,
    random_blocks,
    summary_blocks,
    seg_start,
    seg_end,
):
    tok_rows = tokens.shape[0]
    columns = w_query.shape[1]
    heads = columns // HD
    block_count = tok_rows // BLK
    devices = lax.axis_size("seq")
    groups = lax.axis_size("head")
    me = lax.axis_index("seq")
    group = lax.axis_index("head")
    share = seg_start.shape[0] // devices

    order = np.array(ring_order(devices), np.int32)
    position = jnp.asarray(np.argsort(order).astype(np.int32))[me]
    steps = [0] + [s * k for k in range(1, devices // 2) for s in (-1, 1)] + [devices // 2]
    owner_ids = jnp.asarray(order)[(position + jnp.asarray(steps, jnp.int32)) % devices]
    mine = lax.dynamic_slice_in_dim(random_blocks, me * block_count, block_count, 0)
    table = jnp.concatenate([window_blocks, mine, summary_blocks], axis=1)
    first_segment = lax.rem(me + devices // 2, devices) * share
    start = lax.dynamic_slice_in_dim(seg_start, first_segment, share, 0) - me * tok_rows
    end = lax.dynamic_slice_in_dim(seg_end, first_segment, share, 0) - me * tok_rows

    start, end = start[None, :], end[None, :]
    steps = devices // 2

    def to_head(value, flip):
        return lax.ppermute(value, "head", [(g, g ^ flip) for g in range(groups)])

    turns = [((at, step),) for step in range(steps - 1) for at in (0, 1)]
    turns += [((2, 0),), ((0, steps - 1), (1, steps - 1)), ((3, 0),)]
    turns += [((at, step),) for step in range(1, steps) for at in (2, 3)]
    joined = 2 * steps - 1
    rings = [
        Ring(chunk, devices, way)
        for chunk, way in zip(
            project_kv(tokens, w_key, w_value, start, end, (0, 1)), WAYS[:2], strict=True
        )
    ]
    started, kernels = [], []
    pieces = {}

    def finish(head, *needed):
        own = attend(
            after(table, *needed), owner_ids, queries, rings[head].buffers, head, devices, share
        )
        pieces[0, head] = own
        pieces[1, head] = to_head(own, 1)
        pieces[2, head] = to_head(own, 2)
        if head < heads - 1:
            pieces[3, head] = to_head(pieces[2, head], 1)
        return own

    out_weights = {0: lax.dynamic_slice_in_dim(w_out, group * columns, columns, 1)}
    for turn, moves in enumerate(turns):
        needed = [*(started[-2] if turn > 1 else ()), *(kernels[-1] if turn > 0 else ())]
        begun, ran = [], []
        for head, _ in moves:
            begun += rings[head].step(*needed)
        if turn == 4:
            chunks = project_kv(after(tokens, *needed), w_key, w_value, start, end, (2, 3))
            rings += [
                Ring(chunk, devices, way) for chunk, way in zip(chunks, WAYS[2:], strict=True)
            ]
            ran += chunks
        if turn == 6:
            queries = jnp.dot(after(tokens, *needed), w_query, preferred_element_type=jnp.float32)
            queries = queries.astype(jnp.bfloat16)
            ran.append(queries)
        if turn in (2, 3):
            for flip in ((2,), (3, 1))[(2, 3).index(turn)]:
                part = lax.dynamic_slice_in_dim(
                    after(w_out, *needed), (group ^ flip) * columns, columns, 1
                )
                out_weights[flip] = to_head(part, flip)
                begun.append(out_weights[flip])
        if turn in (joined + 2, joined + 3):
            ran.append(finish(turn - joined - 2, *needed))
        if turn in (joined + 3, joined + 4):
            begun.append(pieces[2, turn - joined - 3])
        if turn == len(turns) - 1:
            ran.append(finish(2, *needed))
        started.append(begun)
        kernels.append(ran)
    finish(3, pieces[0, 2])
    late = [(flip, heads - 1) for flip in (2, 3)]
    early = [place for place in pieces if place not in late]
    total = project_out([pieces[place] for place in early], out_weights, early, None)
    pieces[3, heads - 1] = to_head(after(pieces[2, heads - 1], total), 1)
    return project_out([pieces[place] for place in late], out_weights, late, total)


def solution(mesh):
    placed = (
        P("seq", None),
        P(None, "head"),
        P(None, "head"),
        P(None, "head"),
        P("head", None),
        P("seq", None),
        P(),
        P("seq", None),
        P(),
        P(),
    )
    return jax.shard_map(
        per_device, mesh=mesh, in_specs=placed, out_specs=P("seq", "head"), check_vma=False
    )
```

```python
import functools

import jax
import jax.numpy as jnp
import numpy as np
from jax import lax
from jax.experimental import pallas as pl
from jax.experimental.pallas import tpu as pltpu
from jax.sharding import PartitionSpec as P

HD = 128
BLK = 128
MIB = 1 << 20


def ring_order(devices):
    half = devices // 2
    return [2 * i for i in range(half)] + [2 * i + 1 for i in reversed(range(half))]


def after(value, *others):
    return lax.optimization_barrier((value, others))[0]


def kv_kernel(heads, tokens_ref, wk_ref, wv_ref, start_ref, end_ref, *refs):
    outs = refs[: len(heads)]
    rows_held, weight, sems = refs[len(heads) :]
    tok_rows = tokens_ref.shape[0]
    tiles = 4
    tile = tok_rows // tiles
    columns = weight.shape[1]
    copies = []
    for at, head in enumerate(heads):
        for which, source in enumerate((wk_ref, wv_ref)):
            copies.append(
                pltpu.make_async_copy(
                    source.at[:, pl.ds(head * HD, HD)],
                    weight.at[:, pl.ds((2 * at + which) * HD, HD)],
                    sems.at[len(copies)],
                )
            )
    for at in range(tiles):
        rows = pl.ds(at * tile, tile)
        copies.append(
            pltpu.make_async_copy(tokens_ref.at[rows], rows_held.at[rows], sems.at[len(copies)])
        )
    for copy in copies:
        copy.start()
    for copy in copies[: 2 * len(heads)]:
        copy.wait()
    share = start_ref.shape[1]
    start = start_ref[...]
    end = end_ref[...]
    ones = jnp.ones((tile, HD), jnp.bfloat16)
    sums = jnp.zeros((share, columns), jnp.float32)
    counts = jnp.zeros((share, HD), jnp.float32)
    for at in range(tiles):
        copies[2 * len(heads) + at].wait()
        rows = slice(at * tile, (at + 1) * tile)
        kv = jnp.dot(rows_held[rows, :], weight[...], preferred_element_type=jnp.float32)
        kv = kv.astype(jnp.bfloat16)
        for to, out in enumerate(outs):
            out[rows, :] = kv[:, 2 * to * HD : 2 * (to + 1) * HD]
        position = lax.broadcasted_iota(jnp.int32, (tile, share), 0) + at * tile
        member = (position >= start) & (position < end)
        member = member.astype(jnp.float32).astype(jnp.bfloat16)
        over_rows = (((0,), (0,)), ((), ()))
        sums += lax.dot_general(member, kv, over_rows, preferred_element_type=jnp.float32)
        counts += lax.dot_general(member, ones, over_rows, preferred_element_type=jnp.float32)
    means = (sums / counts[:, :1]).astype(jnp.bfloat16)
    for to, out in enumerate(outs):
        out[tok_rows:, :] = means[:, 2 * to * HD : 2 * (to + 1) * HD]


def project_kv(tokens, w_key, w_value, start, end, heads):
    tok_rows, width = tokens.shape
    share = start.shape[1]
    any_spec = pl.BlockSpec(memory_space=pl.ANY)
    out_shape = (tok_rows + share, 2 * HD)
    return pl.pallas_call(
        functools.partial(kv_kernel, heads),
        grid=(1,),
        in_specs=[any_spec] * 3 + [pl.BlockSpec((1, share), lambda i: (0, 0))] * 2,
        out_specs=[pl.BlockSpec(out_shape, lambda i: (0, 0))] * len(heads),
        out_shape=[jax.ShapeDtypeStruct(out_shape, jnp.bfloat16)] * len(heads),
        scratch_shapes=[
            pltpu.VMEM((tok_rows, width), jnp.bfloat16),
            pltpu.VMEM((width, 2 * HD * len(heads)), jnp.bfloat16),
            pltpu.SemaphoreType.DMA((2 * len(heads) + 4,)),
        ],
        compiler_params=pltpu.CompilerParams(vmem_limit_bytes=60 * MIB),
        cost_estimate=pl.CostEstimate(
            flops=2 * tok_rows * width * 2 * HD * len(heads),
            bytes_accessed=6 * MIB,
            transcendentals=0,
        ),
        name="project_kv",
    )(tokens, w_key, w_value, start, end)


def attend_kernel(devices, table_ref, owner_ref, q_ref, *refs):
    buffers = refs[:-4]
    out_ref, kv, summary, sems = refs[-4:]
    tok_rows = q_ref.shape[0]
    share = summary.shape[0] // devices
    copies = []

    def copy(source, target):
        done = pltpu.make_async_copy(source, target, sems.at[len(copies)])
        done.start()
        copies.append(done)

    for at, buffer in enumerate(buffers):
        owner = owner_ref[min(at, devices - 1)]
        first = buffers[devices - 1].shape[0] if at == devices else 0
        rows = min(buffer.shape[0], tok_rows - first)
        base = pl.multiple_of(owner * tok_rows + first, 16)
        copy(buffer.at[pl.ds(0, rows)], kv.at[pl.ds(base, rows)])
        if buffer.shape[0] > rows:
            segment = lax.rem(owner + devices // 2, devices)
            base = pl.multiple_of(segment * share, 16)
            copy(buffer.at[pl.ds(rows, share)], summary.at[pl.ds(base, share)])
    for done in copies:
        done.wait()
    factor = HD**-0.5 * float(np.log2(np.e))
    slots = table_ref.shape[1]
    for block in range(tok_rows // BLK):
        parts = []
        for slot in range(slots):
            base = pl.multiple_of(table_ref[block, slot] * BLK, BLK)
            source = kv if slot < slots - 2 else summary
            parts.append(source[pl.ds(base, BLK), :])
        gathered = jnp.concatenate(parts, axis=0)
        rows = slice(block * BLK, (block + 1) * BLK)
        scores = lax.dot_general(
            gathered[:, :HD],
            q_ref[rows, :],
            (((1,), (1,)), ((), ())),
            preferred_element_type=jnp.float32,
        )
        peak = jnp.max(scores, axis=0, keepdims=True)
        weights = jnp.exp2((scores - peak) * factor)
        total = jnp.sum(weights, axis=0, keepdims=True)
        mixed = lax.dot_general(
            gathered[:, HD:],
            weights.astype(jnp.bfloat16),
            (((0,), (0,)), ((), ())),
            preferred_element_type=jnp.float32,
        )
        out_ref[rows, :] = (mixed / total).T.astype(jnp.bfloat16)


def attend(table, owner_ids, queries, buffers, head, devices, share):
    tok_rows = queries.shape[0]
    any_spec = pl.BlockSpec(memory_space=pl.ANY)
    smem = pl.BlockSpec(memory_space=pltpu.SMEM)
    return pl.pallas_call(
        functools.partial(attend_kernel, devices),
        grid=(1,),
        in_specs=[smem, smem, pl.BlockSpec((tok_rows, HD), lambda i: (0, head))]
        + [any_spec] * len(buffers),
        out_specs=pl.BlockSpec((tok_rows, HD), lambda i: (0, 0)),
        out_shape=jax.ShapeDtypeStruct((tok_rows, HD), jnp.bfloat16),
        scratch_shapes=[
            pltpu.VMEM((devices * tok_rows, 2 * HD), jnp.bfloat16),
            pltpu.VMEM((devices * share, 2 * HD), jnp.bfloat16),
            pltpu.SemaphoreType.DMA((2 * devices + 1,)),
        ],
        compiler_params=pltpu.CompilerParams(vmem_limit_bytes=48 * MIB),
        cost_estimate=pl.CostEstimate(
            flops=4 * tok_rows * 1152 * HD,
            bytes_accessed=devices * tok_rows * 4 * HD,
            transcendentals=tok_rows * 1152,
        ),
        name="attend",
    )(table, owner_ids, queries, *buffers)


def out_kernel(pieces, final, *refs):
    out_ref = refs[-1]
    rows = jnp.concatenate([ref[...] for ref in refs[:pieces]], axis=1)
    weights = refs[pieces : 2 * pieces]
    weight = jnp.concatenate([ref[...] for ref in weights], axis=0)
    total = jnp.dot(rows, weight, preferred_element_type=jnp.float32)
    if final:
        total += refs[2 * pieces][...]
    out_ref[...] = total.astype(out_ref.dtype)


def project_out(pieces, weights, places, total):
    tok_rows = pieces[0].shape[0]
    columns = weights[0].shape[1]
    final = total is not None
    tile = tok_rows // 2 if final else 512
    row_spec = pl.BlockSpec((tile, columns), lambda i: (i, 0))

    def weight_spec(head):
        return pl.BlockSpec((HD, columns), lambda i: (head, 0))

    return pl.pallas_call(
        functools.partial(out_kernel, len(pieces), final),
        grid=(tok_rows // tile,),
        in_specs=[pl.BlockSpec((tile, HD), lambda i: (i, 0))] * len(pieces)
        + [weight_spec(head) for _, head in places]
        + [row_spec] * final,
        out_specs=row_spec,
        out_shape=jax.ShapeDtypeStruct(
            (tok_rows, columns), jnp.bfloat16 if final else jnp.float32
        ),
        compiler_params=pltpu.CompilerParams(vmem_limit_bytes=63 * MIB),
        cost_estimate=pl.CostEstimate(
            flops=2 * tok_rows * len(pieces) * HD * columns,
            bytes_accessed=6 * MIB,
            transcendentals=0,
        ),
        name="project_out",
    )(*pieces, *[weights[at] for at, _ in places], *([total] if final else []))


WAYS = ("ahead", "behind", "both", "both")


class Ring:
    def __init__(self, chunk, devices, last_way):
        order = ring_order(devices)
        self.forward = [(order[p], order[(p + 1) % devices]) for p in range(devices)]
        self.backward = [(target, source) for source, target in self.forward]
        self.steps = devices // 2
        self.last_way = last_way
        self.buffers = [chunk]
        self.last = (chunk, chunk)

    def step(self, *others):
        ahead, behind = after(self.last, *others)
        ways = ("ahead", "behind")
        if len(self.buffers) == 2 * self.steps - 1:
            if self.last_way in ways:
                ways = (self.last_way,)
            else:
                half = ahead.shape[0] // 32 * 16
                ahead, behind = ahead[:half], behind[half:]
        given = []
        if "ahead" in ways:
            given.append(lax.ppermute(ahead, "seq", self.forward))
        if "behind" in ways:
            given.append(lax.ppermute(behind, "seq", self.backward))
        self.last = given
        self.buffers += given
        return given


def per_device(
    tokens,
    w_query,
    w_key,
    w_value,
    w_out,
    window_blocks,
    random_blocks,
    summary_blocks,
    seg_start,
    seg_end,
):
    tok_rows = tokens.shape[0]
    columns = w_query.shape[1]
    heads = columns // HD
    block_count = tok_rows // BLK
    devices = lax.axis_size("seq")
    groups = lax.axis_size("head")
    me = lax.axis_index("seq")
    group = lax.axis_index("head")
    share = seg_start.shape[0] // devices

    order = np.array(ring_order(devices), np.int32)
    position = jnp.asarray(np.argsort(order).astype(np.int32))[me]
    steps = [0] + [s * k for k in range(1, devices // 2) for s in (-1, 1)] + [devices // 2]
    owner_ids = jnp.asarray(order)[(position + jnp.asarray(steps, jnp.int32)) % devices]
    mine = lax.dynamic_slice_in_dim(random_blocks, me * block_count, block_count, 0)
    table = jnp.concatenate([window_blocks, mine, summary_blocks], axis=1)
    first_segment = lax.rem(me + devices // 2, devices) * share
    start = lax.dynamic_slice_in_dim(seg_start, first_segment, share, 0) - me * tok_rows
    end = lax.dynamic_slice_in_dim(seg_end, first_segment, share, 0) - me * tok_rows

    start, end = start[None, :], end[None, :]
    steps = devices // 2

    def to_head(value, flip):
        return lax.ppermute(value, "head", [(g, g ^ flip) for g in range(groups)])

    turns = [((at, step),) for step in range(steps - 1) for at in (0, 1)]
    turns += [((2, 0),), ((0, steps - 1), (1, steps - 1)), ((3, 0),)]
    turns += [((at, step),) for step in range(1, steps) for at in (2, 3)]
    joined = 2 * steps - 1
    rings = [
        Ring(chunk, devices, way)
        for chunk, way in zip(
            [project_kv(tokens, w_key, w_value, start, end, (head,))[0] for head in (0, 1)],
            WAYS[:2],
            strict=True,
        )
    ]
    started, kernels = [], []
    pieces = {}

    def finish(head, *needed):
        own = attend(
            after(table, *needed), owner_ids, queries, rings[head].buffers, head, devices, share
        )
        pieces[0, head] = own
        pieces[2, head] = to_head(own, 2)
        pieces[1, head] = to_head(own, 1)
        if head < heads - 1:
            pieces[3, head] = to_head(pieces[2, head], 1)
        return own

    out_weights = {}
    for turn, moves in enumerate(turns):
        needed = [*(started[-2] if turn > 1 else ()), *(kernels[-1] if turn > 0 else ())]
        begun, ran = [], []
        for head, _ in moves:
            begun += rings[head].step(*needed)
        if turn == 4:
            chunks = project_kv(after(tokens, *needed), w_key, w_value, start, end, (2, 3))
            rings += [
                Ring(chunk, devices, way) for chunk, way in zip(chunks, WAYS[2:], strict=True)
            ]
            ran += chunks
        if turn == 6:
            queries = jnp.dot(after(tokens, *needed), w_query, preferred_element_type=jnp.float32)
            queries = queries.astype(jnp.bfloat16)
            ran.append(queries)
        if turn in (3, 4):
            for flip in ((2, 0), (3, 1))[(3, 4).index(turn)]:
                part = lax.dynamic_slice_in_dim(
                    after(w_out, *needed), (group ^ flip) * columns, columns, 1
                )
                out_weights[flip] = to_head(part, flip) if flip else part
                begun.append(out_weights[flip])
        if turn in (joined + 2, joined + 3):
            ran.append(finish(turn - joined - 2, *needed))
        if turn in (joined + 3, joined + 3 + 1):
            begun.append(pieces[2, turn - joined - 3])
        if turn == len(turns) - 1:
            ran.append(finish(2, *needed))
        started.append(begun)
        kernels.append(ran)
    finish(3, pieces[0, 2])
    late = [(flip, heads - 1) for flip in (2, 3)]
    early = [place for place in pieces if place not in late]
    total = project_out([pieces[place] for place in early], out_weights, early, None)
    pieces[3, heads - 1] = to_head(after(pieces[2, heads - 1], total), 1)
    return project_out([pieces[place] for place in late], out_weights, late, total)


def solution(mesh):
    placed = (
        P("seq", None),
        P(None, "head"),
        P(None, "head"),
        P(None, "head"),
        P("head", None),
        P("seq", None),
        P(),
        P("seq", None),
        P(),
        P(),
    )
    return jax.shard_map(
        per_device, mesh=mesh, in_specs=placed, out_specs=P("seq", "head"), check_vma=False
    )
```

```python
import functools

import jax
import jax.numpy as jnp
import numpy as np
from jax import lax
from jax.experimental import pallas as pl
from jax.experimental.pallas import tpu as pltpu
from jax.sharding import PartitionSpec as P

HD = 128
BLK = 128
MIB = 1 << 20


def ring_order(devices):
    half = devices // 2
    return [2 * i for i in range(half)] + [2 * i + 1 for i in reversed(range(half))]


def after(value, *others):
    return lax.optimization_barrier((value, others))[0]


def kv_kernel(heads, tokens_ref, wk_ref, wv_ref, start_ref, end_ref, *refs):
    outs = refs[: len(heads)]
    rows_held, weight, sems = refs[len(heads) :]
    tok_rows = tokens_ref.shape[0]
    tiles = 1
    tile = tok_rows // tiles
    columns = weight.shape[1]
    copies = []
    for at, head in enumerate(heads):
        for which, source in enumerate((wk_ref, wv_ref)):
            copies.append(
                pltpu.make_async_copy(
                    source.at[:, pl.ds(head * HD, HD)],
                    weight.at[:, pl.ds((2 * at + which) * HD, HD)],
                    sems.at[len(copies)],
                )
            )
    for at in range(tiles):
        rows = pl.ds(at * tile, tile)
        copies.append(
            pltpu.make_async_copy(tokens_ref.at[rows], rows_held.at[rows], sems.at[len(copies)])
        )
    for copy in copies:
        copy.start()
    for copy in copies[: 2 * len(heads)]:
        copy.wait()
    share = start_ref.shape[1]
    start = start_ref[...]
    end = end_ref[...]
    ones = jnp.ones((tile, HD), jnp.bfloat16)
    sums = jnp.zeros((share, columns), jnp.float32)
    counts = jnp.zeros((share, HD), jnp.float32)
    for at in range(tiles):
        copies[2 * len(heads) + at].wait()
        rows = slice(at * tile, (at + 1) * tile)
        kv = jnp.dot(rows_held[rows, :], weight[...], preferred_element_type=jnp.float32)
        kv = kv.astype(jnp.bfloat16)
        for to, out in enumerate(outs):
            out[rows, :] = kv[:, 2 * to * HD : 2 * (to + 1) * HD]
        position = lax.broadcasted_iota(jnp.int32, (tile, share), 0) + at * tile
        member = (position >= start) & (position < end)
        member = member.astype(jnp.float32).astype(jnp.bfloat16)
        over_rows = (((0,), (0,)), ((), ()))
        sums += lax.dot_general(member, kv, over_rows, preferred_element_type=jnp.float32)
        counts += lax.dot_general(member, ones, over_rows, preferred_element_type=jnp.float32)
    means = (sums / counts[:, :1]).astype(jnp.bfloat16)
    for to, out in enumerate(outs):
        out[tok_rows:, :] = means[:, 2 * to * HD : 2 * (to + 1) * HD]


def project_kv(tokens, w_key, w_value, start, end, heads):
    tok_rows, width = tokens.shape
    share = start.shape[1]
    any_spec = pl.BlockSpec(memory_space=pl.ANY)
    out_shape = (tok_rows + share, 2 * HD)
    return pl.pallas_call(
        functools.partial(kv_kernel, heads),
        grid=(1,),
        in_specs=[any_spec] * 3 + [pl.BlockSpec((1, share), lambda i: (0, 0))] * 2,
        out_specs=[pl.BlockSpec(out_shape, lambda i: (0, 0))] * len(heads),
        out_shape=[jax.ShapeDtypeStruct(out_shape, jnp.bfloat16)] * len(heads),
        scratch_shapes=[
            pltpu.VMEM((tok_rows, width), jnp.bfloat16),
            pltpu.VMEM((width, 2 * HD * len(heads)), jnp.bfloat16),
            pltpu.SemaphoreType.DMA((2 * len(heads) + 1,)),
        ],
        compiler_params=pltpu.CompilerParams(vmem_limit_bytes=60 * MIB),
        cost_estimate=pl.CostEstimate(
            flops=2 * tok_rows * width * 2 * HD * len(heads),
            bytes_accessed=6 * MIB,
            transcendentals=0,
        ),
        name="project_kv",
    )(tokens, w_key, w_value, start, end)


def attend_kernel(devices, table_ref, owner_ref, q_ref, *refs):
    buffers = refs[:-4]
    out_ref, kv, summary, sems = refs[-4:]
    tok_rows = q_ref.shape[0]
    share = summary.shape[0] // devices
    copies = []

    def copy(source, target):
        done = pltpu.make_async_copy(source, target, sems.at[len(copies)])
        done.start()
        copies.append(done)

    for at, buffer in enumerate(buffers):
        owner = owner_ref[min(at, devices - 1)]
        first = buffers[devices - 1].shape[0] if at == devices else 0
        rows = min(buffer.shape[0], tok_rows - first)
        base = pl.multiple_of(owner * tok_rows + first, 16)
        copy(buffer.at[pl.ds(0, rows)], kv.at[pl.ds(base, rows)])
        if buffer.shape[0] > rows:
            segment = lax.rem(owner + devices // 2, devices)
            base = pl.multiple_of(segment * share, 16)
            copy(buffer.at[pl.ds(rows, share)], summary.at[pl.ds(base, share)])
    for done in copies:
        done.wait()
    factor = HD**-0.5 * float(np.log2(np.e))
    slots = table_ref.shape[1]
    for block in range(tok_rows // BLK):
        parts = []
        for slot in range(slots):
            base = pl.multiple_of(table_ref[block, slot] * BLK, BLK)
            source = kv if slot < slots - 2 else summary
            parts.append(source[pl.ds(base, BLK), :])
        gathered = jnp.concatenate(parts, axis=0)
        rows = slice(block * BLK, (block + 1) * BLK)
        scores = lax.dot_general(
            gathered[:, :HD],
            q_ref[rows, :],
            (((1,), (1,)), ((), ())),
            preferred_element_type=jnp.float32,
        )
        peak = jnp.max(scores, axis=0, keepdims=True)
        weights = jnp.exp2((scores - peak) * factor)
        total = jnp.sum(weights, axis=0, keepdims=True)
        mixed = lax.dot_general(
            gathered[:, HD:],
            weights.astype(jnp.bfloat16),
            (((0,), (0,)), ((), ())),
            preferred_element_type=jnp.float32,
        )
        out_ref[rows, :] = (mixed / total).T.astype(jnp.bfloat16)


def attend(table, owner_ids, queries, buffers, head, devices, share):
    tok_rows = queries.shape[0]
    any_spec = pl.BlockSpec(memory_space=pl.ANY)
    smem = pl.BlockSpec(memory_space=pltpu.SMEM)
    return pl.pallas_call(
        functools.partial(attend_kernel, devices),
        grid=(1,),
        in_specs=[smem, smem, pl.BlockSpec((tok_rows, HD), lambda i: (0, head))]
        + [any_spec] * len(buffers),
        out_specs=pl.BlockSpec((tok_rows, HD), lambda i: (0, 0)),
        out_shape=jax.ShapeDtypeStruct((tok_rows, HD), jnp.bfloat16),
        scratch_shapes=[
            pltpu.VMEM((devices * tok_rows, 2 * HD), jnp.bfloat16),
            pltpu.VMEM((devices * share, 2 * HD), jnp.bfloat16),
            pltpu.SemaphoreType.DMA((2 * devices + 1,)),
        ],
        compiler_params=pltpu.CompilerParams(vmem_limit_bytes=(60 if head < 2 else 24) * MIB),
        cost_estimate=pl.CostEstimate(
            flops=4 * tok_rows * 1152 * HD,
            bytes_accessed=devices * tok_rows * 4 * HD,
            transcendentals=tok_rows * 1152,
        ),
        name="attend",
    )(table, owner_ids, queries, *buffers)


def out_kernel(pieces, final, *refs):
    out_ref = refs[-1]
    rows = jnp.concatenate([ref[...] for ref in refs[:pieces]], axis=1)
    weights = refs[pieces : 2 * pieces]
    weight = jnp.concatenate([ref[...] for ref in weights], axis=0)
    total = jnp.dot(rows, weight, preferred_element_type=jnp.float32)
    if final:
        total += refs[2 * pieces][...]
    out_ref[...] = total.astype(out_ref.dtype)


def project_out(pieces, weights, places, total):
    tok_rows = pieces[0].shape[0]
    columns = weights[0].shape[1]
    final = total is not None
    tile = tok_rows // 2 if final else 512
    row_spec = pl.BlockSpec((tile, columns), lambda i: (i, 0))

    def weight_spec(head):
        return pl.BlockSpec((HD, columns), lambda i: (head, 0))

    return pl.pallas_call(
        functools.partial(out_kernel, len(pieces), final),
        grid=(tok_rows // tile,),
        in_specs=[pl.BlockSpec((tile, HD), lambda i: (i, 0))] * len(pieces)
        + [weight_spec(head) for _, head in places]
        + [row_spec] * final,
        out_specs=row_spec,
        out_shape=jax.ShapeDtypeStruct(
            (tok_rows, columns), jnp.bfloat16 if final else jnp.float32
        ),
        compiler_params=pltpu.CompilerParams(vmem_limit_bytes=24 * MIB),
        cost_estimate=pl.CostEstimate(
            flops=2 * tok_rows * len(pieces) * HD * columns,
            bytes_accessed=6 * MIB,
            transcendentals=0,
        ),
        name="project_out",
    )(*pieces, *[weights[at] for at, _ in places], *([total] if final else []))


WAYS = ("ahead", "behind", "both", "both")


class Ring:
    def __init__(self, chunk, devices, last_way):
        order = ring_order(devices)
        self.forward = [(order[p], order[(p + 1) % devices]) for p in range(devices)]
        self.backward = [(target, source) for source, target in self.forward]
        self.steps = devices // 2
        self.last_way = last_way
        self.buffers = [chunk]
        self.last = (chunk, chunk)

    def step(self, *others):
        ahead, behind = after(self.last, *others)
        ways = ("ahead", "behind")
        if len(self.buffers) == 2 * self.steps - 1:
            if self.last_way in ways:
                ways = (self.last_way,)
            else:
                half = ahead.shape[0] // 32 * 16
                ahead, behind = ahead[:half], behind[half:]
        given = []
        if "ahead" in ways:
            given.append(lax.ppermute(ahead, "seq", self.forward))
        if "behind" in ways:
            given.append(lax.ppermute(behind, "seq", self.backward))
        self.last = given
        self.buffers += given
        return given


def per_device(
    tokens,
    w_query,
    w_key,
    w_value,
    w_out,
    window_blocks,
    random_blocks,
    summary_blocks,
    seg_start,
    seg_end,
):
    tok_rows = tokens.shape[0]
    columns = w_query.shape[1]
    heads = columns // HD
    block_count = tok_rows // BLK
    devices = lax.axis_size("seq")
    groups = lax.axis_size("head")
    me = lax.axis_index("seq")
    group = lax.axis_index("head")
    share = seg_start.shape[0] // devices

    order = np.array(ring_order(devices), np.int32)
    position = jnp.asarray(np.argsort(order).astype(np.int32))[me]
    steps = [0] + [s * k for k in range(1, devices // 2) for s in (-1, 1)] + [devices // 2]
    owner_ids = jnp.asarray(order)[(position + jnp.asarray(steps, jnp.int32)) % devices]
    mine = lax.dynamic_slice_in_dim(random_blocks, me * block_count, block_count, 0)
    table = jnp.concatenate([window_blocks, mine, summary_blocks], axis=1)
    first_segment = lax.rem(me + devices // 2, devices) * share
    start = lax.dynamic_slice_in_dim(seg_start, first_segment, share, 0) - me * tok_rows
    end = lax.dynamic_slice_in_dim(seg_end, first_segment, share, 0) - me * tok_rows

    start, end = start[None, :], end[None, :]
    steps = devices // 2

    def to_head(value, flip):
        return lax.ppermute(value, "head", [(g, g ^ flip) for g in range(groups)])

    turns = [((at, step),) for step in range(steps - 1) for at in (0, 1)]
    turns += [((2, 0),), ((0, steps - 1), (1, steps - 1)), ((3, 0),)]
    turns += [((at, step),) for step in range(1, steps) for at in (2, 3)]
    joined = 2 * steps - 1
    rings = [
        Ring(chunk, devices, way)
        for chunk, way in zip(
            [project_kv(tokens, w_key, w_value, start, end, (head,))[0] for head in (0, 1)],
            WAYS[:2],
            strict=True,
        )
    ]
    started, kernels = [], []
    pieces = {}

    def finish(head, *needed):
        own = attend(
            after(table, *needed), owner_ids, queries, rings[head].buffers, head, devices, share
        )
        pieces[0, head] = own
        pieces[2, head] = to_head(own, 2)
        pieces[1, head] = to_head(own, 1)
        if head < heads - 1:
            pieces[3, head] = to_head(pieces[2, head], 1)
        return own

    out_weights = {}
    for turn, moves in enumerate(turns):
        needed = [*(started[-2] if turn > 1 else ()), *(kernels[-1] if turn > 0 else ())]
        begun, ran = [], []
        for head, _ in moves:
            begun += rings[head].step(*needed)
        if turn == 4:
            chunks = project_kv(after(tokens, *needed), w_key, w_value, start, end, (2, 3))
            rings += [
                Ring(chunk, devices, way) for chunk, way in zip(chunks, WAYS[2:], strict=True)
            ]
            ran += chunks
        if turn == 6:
            queries = jnp.dot(after(tokens, *needed), w_query, preferred_element_type=jnp.float32)
            queries = queries.astype(jnp.bfloat16)
            ran.append(queries)
        if turn in (3, 4):
            for flip in ((2, 0), (3, 1))[(3, 4).index(turn)]:
                part = lax.dynamic_slice_in_dim(
                    after(w_out, *needed), (group ^ flip) * columns, columns, 1
                )
                out_weights[flip] = to_head(part, flip) if flip else part
                begun.append(out_weights[flip])
        if turn in (joined + 2, joined + 3):
            ran.append(finish(turn - joined - 2, *needed))
        if turn in (joined + 3, joined + 3 + 1):
            begun.append(pieces[2, turn - joined - 3])
        if turn == len(turns) - 1:
            ran.append(finish(2, *needed))
        started.append(begun)
        kernels.append(ran)
    finish(3, pieces[0, 2])
    late = [(flip, heads - 1) for flip in (2, 3)]
    early = [place for place in pieces if place not in late]
    total = project_out([pieces[place] for place in early], out_weights, early, None)
    pieces[3, heads - 1] = to_head(after(pieces[2, heads - 1], total), 1)
    return project_out([pieces[place] for place in late], out_weights, late, total)


def solution(mesh):
    placed = (
        P("seq", None),
        P(None, "head"),
        P(None, "head"),
        P(None, "head"),
        P("head", None),
        P("seq", None),
        P(),
        P("seq", None),
        P(),
        P(),
    )
    return jax.shard_map(
        per_device, mesh=mesh, in_specs=placed, out_specs=P("seq", "head"), check_vma=False
    )
```

```python
import functools

import jax
import jax.numpy as jnp
import numpy as np
from jax import lax
from jax.experimental import pallas as pl
from jax.experimental.pallas import tpu as pltpu
from jax.sharding import PartitionSpec as P

HD = 128
BLK = 128
MIB = 1 << 20


def ring_order(devices):
    half = devices // 2
    return [2 * i for i in range(half)] + [2 * i + 1 for i in reversed(range(half))]


def after(value, *others):
    return lax.optimization_barrier((value, others))[0]


def kv_kernel(heads, tokens_ref, wk_ref, wv_ref, start_ref, end_ref, *refs):
    outs = refs[: len(heads)]
    rows_held, weight, sems = refs[len(heads) :]
    tok_rows = tokens_ref.shape[0]
    tiles = 1
    tile = tok_rows // tiles
    columns = weight.shape[1]
    copies = []
    for at, head in enumerate(heads):
        for which, source in enumerate((wk_ref, wv_ref)):
            copies.append(
                pltpu.make_async_copy(
                    source.at[:, pl.ds(head * HD, HD)],
                    weight.at[:, pl.ds((2 * at + which) * HD, HD)],
                    sems.at[len(copies)],
                )
            )
    for at in range(tiles):
        rows = pl.ds(at * tile, tile)
        copies.append(
            pltpu.make_async_copy(tokens_ref.at[rows], rows_held.at[rows], sems.at[len(copies)])
        )
    for copy in copies:
        copy.start()
    for copy in copies[: 2 * len(heads)]:
        copy.wait()
    share = start_ref.shape[1]
    start = start_ref[...]
    end = end_ref[...]
    sums = jnp.zeros((share, columns), jnp.float32)
    counts = jnp.broadcast_to((end - start).astype(jnp.float32), (HD, share)).T
    for at in range(tiles):
        copies[2 * len(heads) + at].wait()
        rows = slice(at * tile, (at + 1) * tile)
        kv = jnp.dot(rows_held[rows, :], weight[...], preferred_element_type=jnp.float32)
        kv = kv.astype(jnp.bfloat16)
        for to, out in enumerate(outs):
            out[rows, :] = kv[:, 2 * to * HD : 2 * (to + 1) * HD]
        position = lax.broadcasted_iota(jnp.int32, (tile, share), 0) + at * tile
        member = (position >= start) & (position < end)
        member = member.astype(jnp.float32).astype(jnp.bfloat16)
        over_rows = (((0,), (0,)), ((), ()))
        sums += lax.dot_general(member, kv, over_rows, preferred_element_type=jnp.float32)
    means = (sums / counts[:, :1]).astype(jnp.bfloat16)
    for to, out in enumerate(outs):
        out[tok_rows:, :] = means[:, 2 * to * HD : 2 * (to + 1) * HD]


def project_kv(tokens, w_key, w_value, start, end, heads):
    tok_rows, width = tokens.shape
    share = start.shape[1]
    any_spec = pl.BlockSpec(memory_space=pl.ANY)
    out_shape = (tok_rows + share, 2 * HD)
    return pl.pallas_call(
        functools.partial(kv_kernel, heads),
        grid=(1,),
        in_specs=[any_spec] * 3 + [pl.BlockSpec((1, share), lambda i: (0, 0))] * 2,
        out_specs=[pl.BlockSpec(out_shape, lambda i: (0, 0))] * len(heads),
        out_shape=[jax.ShapeDtypeStruct(out_shape, jnp.bfloat16)] * len(heads),
        scratch_shapes=[
            pltpu.VMEM((tok_rows, width), jnp.bfloat16),
            pltpu.VMEM((width, 2 * HD * len(heads)), jnp.bfloat16),
            pltpu.SemaphoreType.DMA((2 * len(heads) + 1,)),
        ],
        compiler_params=pltpu.CompilerParams(vmem_limit_bytes=60 * MIB),
        cost_estimate=pl.CostEstimate(
            flops=2 * tok_rows * width * 2 * HD * len(heads),
            bytes_accessed=6 * MIB,
            transcendentals=0,
        ),
        name="project_kv",
    )(tokens, w_key, w_value, start, end)


def attend_kernel(devices, table_ref, owner_ref, q_ref, *refs):
    buffers = refs[:-4]
    out_ref, kv, summary, sems = refs[-4:]
    tok_rows = q_ref.shape[0]
    share = summary.shape[0] // devices
    copies = []

    def copy(source, target):
        done = pltpu.make_async_copy(source, target, sems.at[len(copies)])
        done.start()
        copies.append(done)

    for at, buffer in enumerate(buffers):
        owner = owner_ref[min(at, devices - 1)]
        first = buffers[devices - 1].shape[0] if at == devices else 0
        rows = min(buffer.shape[0], tok_rows - first)
        base = pl.multiple_of(owner * tok_rows + first, 16)
        copy(buffer.at[pl.ds(0, rows)], kv.at[pl.ds(base, rows)])
        if buffer.shape[0] > rows:
            segment = lax.rem(owner + devices // 2, devices)
            base = pl.multiple_of(segment * share, 16)
            copy(buffer.at[pl.ds(rows, share)], summary.at[pl.ds(base, share)])
    for done in copies:
        done.wait()
    factor = HD**-0.5 * float(np.log2(np.e))
    slots = table_ref.shape[1]
    for block in range(tok_rows // BLK):
        parts = []
        for slot in range(slots):
            base = pl.multiple_of(table_ref[block, slot] * BLK, BLK)
            source = kv if slot < slots - 2 else summary
            parts.append(source[pl.ds(base, BLK), :])
        gathered = jnp.concatenate(parts, axis=0)
        rows = slice(block * BLK, (block + 1) * BLK)
        scores = lax.dot_general(
            gathered[:, :HD],
            q_ref[rows, :],
            (((1,), (1,)), ((), ())),
            preferred_element_type=jnp.float32,
        )
        peak = jnp.max(scores, axis=0, keepdims=True)
        weights = jnp.exp2((scores - peak) * factor)
        total = jnp.sum(weights, axis=0, keepdims=True)
        mixed = lax.dot_general(
            gathered[:, HD:],
            weights.astype(jnp.bfloat16),
            (((0,), (0,)), ((), ())),
            preferred_element_type=jnp.float32,
        )
        out_ref[rows, :] = (mixed / total).T.astype(jnp.bfloat16)


def attend(table, owner_ids, queries, buffers, head, devices, share):
    tok_rows = queries.shape[0]
    any_spec = pl.BlockSpec(memory_space=pl.ANY)
    smem = pl.BlockSpec(memory_space=pltpu.SMEM)
    return pl.pallas_call(
        functools.partial(attend_kernel, devices),
        grid=(1,),
        in_specs=[smem, smem, pl.BlockSpec((tok_rows, HD), lambda i: (0, head))]
        + [any_spec] * len(buffers),
        out_specs=pl.BlockSpec((tok_rows, HD), lambda i: (0, 0)),
        out_shape=jax.ShapeDtypeStruct((tok_rows, HD), jnp.bfloat16),
        scratch_shapes=[
            pltpu.VMEM((devices * tok_rows, 2 * HD), jnp.bfloat16),
            pltpu.VMEM((devices * share, 2 * HD), jnp.bfloat16),
            pltpu.SemaphoreType.DMA((2 * devices + 1,)),
        ],
        compiler_params=pltpu.CompilerParams(vmem_limit_bytes=(60 if head < 2 else 24) * MIB),
        cost_estimate=pl.CostEstimate(
            flops=4 * tok_rows * 1152 * HD,
            bytes_accessed=devices * tok_rows * 4 * HD,
            transcendentals=tok_rows * 1152,
        ),
        name="attend",
    )(table, owner_ids, queries, *buffers)


def out_kernel(pieces, final, *refs):
    out_ref = refs[-1]
    rows = jnp.concatenate([ref[...] for ref in refs[:pieces]], axis=1)
    weights = refs[pieces : 2 * pieces]
    weight = jnp.concatenate([ref[...] for ref in weights], axis=0)
    total = jnp.dot(rows, weight, preferred_element_type=jnp.float32)
    if final:
        total += refs[2 * pieces][...]
    out_ref[...] = total.astype(out_ref.dtype)


def project_out(pieces, weights, places, total):
    tok_rows = pieces[0].shape[0]
    columns = weights[0].shape[1]
    final = total is not None
    tile = tok_rows if final else tok_rows
    row_spec = pl.BlockSpec((tile, columns), lambda i: (i, 0))

    def weight_spec(head):
        return pl.BlockSpec((HD, columns), lambda i: (head, 0))

    return pl.pallas_call(
        functools.partial(out_kernel, len(pieces), final),
        grid=(tok_rows // tile,),
        in_specs=[pl.BlockSpec((tile, HD), lambda i: (i, 0))] * len(pieces)
        + [weight_spec(head) for _, head in places]
        + [row_spec] * final,
        out_specs=row_spec,
        out_shape=jax.ShapeDtypeStruct(
            (tok_rows, columns), jnp.bfloat16 if final else jnp.float32
        ),
        compiler_params=pltpu.CompilerParams(vmem_limit_bytes=24 * MIB),
        cost_estimate=pl.CostEstimate(
            flops=2 * tok_rows * len(pieces) * HD * columns,
            bytes_accessed=6 * MIB,
            transcendentals=0,
        ),
        name="project_out",
    )(*pieces, *[weights[at] for at, _ in places], *([total] if final else []))


WAYS = ("ahead", "behind", "both", "both")


class Ring:
    def __init__(self, chunk, devices, last_way):
        order = ring_order(devices)
        self.forward = [(order[p], order[(p + 1) % devices]) for p in range(devices)]
        self.backward = [(target, source) for source, target in self.forward]
        self.steps = devices // 2
        self.last_way = last_way
        self.buffers = [chunk]
        self.last = (chunk, chunk)

    def step(self, *others):
        ahead, behind = after(self.last, *others)
        ways = ("ahead", "behind")
        if len(self.buffers) == 2 * self.steps - 1:
            if self.last_way in ways:
                ways = (self.last_way,)
            else:
                half = ahead.shape[0] // 32 * 16
                ahead, behind = ahead[:half], behind[half:]
        given = []
        if "ahead" in ways:
            given.append(lax.ppermute(ahead, "seq", self.forward))
        if "behind" in ways:
            given.append(lax.ppermute(behind, "seq", self.backward))
        self.last = given
        self.buffers += given
        return given


def per_device(
    tokens,
    w_query,
    w_key,
    w_value,
    w_out,
    window_blocks,
    random_blocks,
    summary_blocks,
    seg_start,
    seg_end,
):
    tok_rows = tokens.shape[0]
    columns = w_query.shape[1]
    heads = columns // HD
    block_count = tok_rows // BLK
    devices = lax.axis_size("seq")
    groups = lax.axis_size("head")
    me = lax.axis_index("seq")
    group = lax.axis_index("head")
    share = seg_start.shape[0] // devices

    order = np.array(ring_order(devices), np.int32)
    position = jnp.asarray(np.argsort(order).astype(np.int32))[me]
    steps = [0] + [s * k for k in range(1, devices // 2) for s in (-1, 1)] + [devices // 2]
    owner_ids = jnp.asarray(order)[(position + jnp.asarray(steps, jnp.int32)) % devices]
    mine = lax.dynamic_slice_in_dim(random_blocks, me * block_count, block_count, 0)
    table = jnp.concatenate([window_blocks, mine, summary_blocks], axis=1)
    first_segment = lax.rem(me + devices // 2, devices) * share
    start = lax.dynamic_slice_in_dim(seg_start, first_segment, share, 0) - me * tok_rows
    end = lax.dynamic_slice_in_dim(seg_end, first_segment, share, 0) - me * tok_rows

    start, end = start[None, :], end[None, :]
    steps = devices // 2

    def to_head(value, flip):
        return lax.ppermute(value, "head", [(g, g ^ flip) for g in range(groups)])

    turns = [((at, step),) for step in range(steps - 1) for at in (0, 1)]
    turns += [((2, 0),), ((0, steps - 1), (1, steps - 1)), ((3, 0),)]
    turns += [((at, step),) for step in range(1, steps) for at in (2, 3)]
    joined = 2 * steps - 1
    rings = [
        Ring(chunk, devices, way)
        for chunk, way in zip(
            [project_kv(tokens, w_key, w_value, start, end, (head,))[0] for head in (0, 1)],
            WAYS[:2],
            strict=True,
        )
    ]
    started, kernels = [], []
    pieces = {}

    def finish(head, *needed):
        own = attend(
            after(table, *needed), owner_ids, queries, rings[head].buffers, head, devices, share
        )
        pieces[0, head] = own
        pieces[2, head] = to_head(own, 2)
        pieces[1, head] = to_head(own, 1)
        if head < heads - 1:
            pieces[3, head] = to_head(pieces[2, head], 1)
        return own

    out_weights = {}
    for turn, moves in enumerate(turns):
        needed = [*(started[-2] if turn > 1 else ()), *(kernels[-1] if turn > 0 else ())]
        begun, ran = [], []
        for head, _ in moves:
            begun += rings[head].step(*needed)
        if turn == 4:
            chunks = project_kv(after(tokens, *needed), w_key, w_value, start, end, (2, 3))
            rings += [
                Ring(chunk, devices, way) for chunk, way in zip(chunks, WAYS[2:], strict=True)
            ]
            ran += chunks
        if turn == 6:
            queries = jnp.dot(after(tokens, *needed), w_query, preferred_element_type=jnp.float32)
            queries = queries.astype(jnp.bfloat16)
            ran.append(queries)
        if turn in (3, 4):
            for flip in ((2, 0), (3, 1))[(3, 4).index(turn)]:
                part = lax.dynamic_slice_in_dim(
                    after(w_out, *needed), (group ^ flip) * columns, columns, 1
                )
                out_weights[flip] = to_head(part, flip) if flip else part
                begun.append(out_weights[flip])
        if turn in (joined + 2, joined + 3):
            ran.append(finish(turn - joined - 2, *needed))
        if turn in (joined + 3, joined + 3 + 1):
            begun.append(pieces[2, turn - joined - 3])
        if turn == len(turns) - 1:
            ran.append(finish(2, *needed))
        started.append(begun)
        kernels.append(ran)
    finish(3, pieces[0, 2])
    late = [(flip, heads - 1) for flip in (2, 3)]
    early = [place for place in pieces if place not in late]
    total = project_out([pieces[place] for place in early], out_weights, early, None)
    pieces[3, heads - 1] = to_head(after(pieces[2, heads - 1], total), 1)
    return project_out([pieces[place] for place in late], out_weights, late, total)


def solution(mesh):
    placed = (
        P("seq", None),
        P(None, "head"),
        P(None, "head"),
        P(None, "head"),
        P("head", None),
        P("seq", None),
        P(),
        P("seq", None),
        P(),
        P(),
    )
    return jax.shard_map(
        per_device, mesh=mesh, in_specs=placed, out_specs=P("seq", "head"), check_vma=False
    )
```
